256 devices in a mesh: wide: 32 (over y, z_hi, x), narrow: 8 (over z_lo, core).
Axes of the slice: x: 4, y: 4, z: 8 (z_hi: 2, z_lo: 4; z = z_hi * 4 + z_lo), core: 2. Of those that a mesh axis runs over, the one named last changes fastest.
Arguments:
- positions: float32 [32, 8, 3, 2048], P('wide', 'narrow'), may hold values from 0 to 3
- velocities: float32 [32, 8, 3, 2048], P('wide', 'narrow'), may hold values from -3 to 3
- charges: float32 [32, 8, 2048], P('wide', 'narrow'), may hold values from -2.5 to 2.5
- radii: float32 [32, 8, 2048], P('wide', 'narrow'), may hold values from 0.12 to 0.2
- tile_pairs: int32 [32, 8, 2, 256], P('wide', 'narrow'), may hold values from 0 to 79, as said below
- tile_counts: int32 [32, 8], P('wide', 'narrow'), may hold values from 64 to 256, as said below
- destinations: int32 [32, 8, 2048], P('wide', 'narrow'), may hold values from 0 to 8, as said below
Outputs:
- positions_out: float32 [32, 8, 3, 2048], P('wide', 'narrow')
- velocities_out: float32 [32, 8, 3, 2048], P('wide', 'narrow')
- born_radii: float32 [32, 8, 2048], P('wide', 'narrow')
- arrivals: float32 [32, 8, 8, 6, 64], P('wide', 'narrow')
- max_shift: float32 [3], replicated
The draws below stay inside these ranges and needn't reach their ends.
Inputs may be any that keep to these rules, and one draw needn't show every extreme that they name: `tile_pairs`: in each brick the entries are distinct pairs (local tile, source tile) with local tiles below 16; a source tile below 16 is never below the local tile of its entry. `tile_counts`: 256 is reached in every draw. `destinations`: 0 keeps an atom in its brick; k from 1 to 8 sends it to the brick at the k-th offset of (-1,-1), (-1,0), (-1,1), (0,-1), (0,1), (1,-1), (1,0), (1,1) along (wide, narrow), wrapping around. At most 64 atoms of one brick take one code, and in every draw some brick sends exactly 64 with some code.
All inputs are finite; a program needn't handle non-finite values.
Results may differ from the reference program's by a relative error of at most 0.0003.
Values sent between devices are 32-bit elements; how exact they have to be, the bound alone decides.
No kernel may reach another device: no remote copies, remote signals or barrier semaphores. Data moves between devices by JAX's collectives and lax.ppermute only.
A program may use at most 64 MiB of HBM per device.

```python
import math
import jax
import jax.numpy as jnp
from jax import lax

ATOMS_DEV = 2048
TILE_PAIRS = 256
MIGRANTS = 64
STEPS = 3
BRICKS_W = 32
BRICKS_N = 8


def draw_tile_pairs(key, part):
    key = jax.random.fold_in(key, 11)
    tile_count = ATOMS_DEV // 128
    total = tile_count * 5 * tile_count
    candidate = jnp.arange(total, dtype=jnp.int32)
    local_part = candidate // (5 * tile_count)
    source_part = candidate % (5 * tile_count)
    invalid = ((source_part < tile_count) & (source_part < local_part)).astype(jnp.int32)

    def one_brick(brick_key):
        ranking = jax.random.permutation(brick_key, total).astype(jnp.int32)
        scores = invalid * total + ranking
        chosen = jnp.argsort(scores, stable=True)[:TILE_PAIRS]
        return jnp.stack([local_part[chosen], source_part[chosen]]).astype(jnp.int32)
    brick_keys = jax.random.split(key, BRICKS_W * BRICKS_N)
    return jax.vmap(one_brick)(brick_keys).reshape(BRICKS_W, BRICKS_N, 2, TILE_PAIRS)


def draw_tile_counts(key, part):
    key = jax.random.fold_in(key, 12)
    key_base, key_heavy, key_pick = jax.random.split(key, 3)
    bricks = BRICKS_W * BRICKS_N
    baseline = jax.random.randint(key_base, (bricks,), TILE_PAIRS // 4, TILE_PAIRS // 2 + 1)
    crowded = jax.random.randint(key_heavy, (bricks,), 0, 8) == 0
    chosen = jax.random.randint(key_pick, (), 0, bricks)
    saturated = crowded | (jnp.arange(bricks, dtype=jnp.int32) == chosen)
    return jnp.where(saturated, TILE_PAIRS, baseline).astype(jnp.int32).reshape(BRICKS_W, BRICKS_N)


def mix_row(row_key, labels):
    return labels[jax.random.permutation(row_key, ATOMS_DEV)]


def draw_destinations(key, part):
    key = jax.random.fold_in(key, 13)
    key_count, key_pick, key_order = jax.random.split(key, 3)
    bricks = BRICKS_W * BRICKS_N
    leaving = jax.random.randint(key_count, (bricks, 8), MIGRANTS // 3, MIGRANTS + 1)
    chosen = jax.random.randint(key_pick, (), 0, bricks * 8)
    flat_index = jnp.arange(bricks * 8, dtype=jnp.int32).reshape(bricks, 8)
    leaving = jnp.where(flat_index == chosen, MIGRANTS, leaving).astype(jnp.int32)
    bounds = jnp.cumsum(leaving, axis=1).astype(jnp.int32)
    position = jnp.arange(ATOMS_DEV, dtype=jnp.int32)
    passed = jnp.sum((position[None, None, :] >= bounds[:, :, None]).astype(jnp.int32), axis=1).astype(jnp.int32)
    labels = jnp.where(passed == 8, 0, passed + 1).astype(jnp.int32)
    order_keys = jax.random.split(key_order, bricks)
    shuffled = jax.vmap(mix_row)(order_keys, labels)
    return shuffled.astype(jnp.int32).reshape(BRICKS_W, BRICKS_N, ATOMS_DEV)


def level_of(own_key, extent, cuts, least, high):
    factor_of, own = 1.0, jax.random.fold_in(own_key, 6)
    for axis_at, parts in cuts:
        steps = jnp.exp(jax.random.uniform(jax.random.fold_in(own, axis_at), (parts,), jnp.float32, least / len(cuts), high / len(cuts)))
        factor_of = factor_of * jnp.repeat(steps, extent[axis_at] // parts).reshape([-1 if axis == axis_at else 1 for axis in range(len(extent))])
    return factor_of


def scatter_about(own_key, shape, spread, reach, pieces=(), held_as=jnp.bfloat16):
    values = spread * jax.random.normal(own_key, shape, jnp.float32)
    if pieces:
        values = values * level_of(own_key, shape, pieces, -0.22, 0.18)
    return jnp.clip(values, -reach, reach).astype(held_as)


def setup_inputs(seed: int = 0) -> dict:
    splits = jax.random.split(jax.random.key(seed), 8)
    positions = jnp.clip(3.0 * jax.random.uniform(splits[0], (BRICKS_W, BRICKS_N, 3, ATOMS_DEV), jnp.float32) ** level_of(splits[0], (BRICKS_W, BRICKS_N, 3, ATOMS_DEV), ((0, 32), (1, 8)), -0.2, 0.2), 0.0, 3.0)
    velocities = scatter_about(splits[1], (BRICKS_W, BRICKS_N, 3, ATOMS_DEV), 0.5, 3.0, ((0, 32), (1, 8)), jnp.float32)
    charges = scatter_about(splits[2], (BRICKS_W, BRICKS_N, ATOMS_DEV), 0.5, 2.5, ((0, 32), (1, 8)), jnp.float32)
    radii = jnp.clip(jnp.exp(math.log(0.2) - 0.51082566 * jax.random.uniform(splits[3], (BRICKS_W, BRICKS_N, ATOMS_DEV), jnp.float32) ** level_of(splits[3], (BRICKS_W, BRICKS_N, ATOMS_DEV), ((0, 32), (1, 8)), -0.2, 0.2)), 0.12, 0.2)
    tile_pairs = draw_tile_pairs(jax.random.fold_in(splits[7], 71), 0)
    tile_counts = draw_tile_counts(jax.random.fold_in(splits[7], 71), 0)
    destinations = draw_destinations(jax.random.fold_in(splits[7], 71), 0)
    return dict(positions=positions, velocities=velocities, charges=charges, radii=radii, tile_pairs=tile_pairs, tile_counts=tile_counts, destinations=destinations)


cutoff_radius = 2.5
skin_depth = 0.2
brick_side = 3.0
step_time = 0.1
coulomb_factor = 0.5
screen_factor = 0.3
half_shell = ((0, 0), (1, -1), (1, 0), (1, 1), (0, 1))
neighbour_offsets = ((-1, -1), (-1, 0), (-1, 1), (0, -1), (0, 1), (1, -1), (1, 0), (1, 1))

def cutoff_switch(squared):
    inner = jnp.maximum(1.0 - squared / (cutoff_radius * cutoff_radius), 0.0)
    return (inner * inner, -2.0 * inner / (cutoff_radius * cutoff_radius))

def separation(first_tile, second_tile):
    displace = first_tile[0:3, :, None] - second_tile[0:3, None, :]
    return (displace, lax.optimization_barrier(jnp.sum(displace * displace, axis=0)))

def screen_pair(first_tile, second_tile, pair_mask):
    displace, squared = separation(first_tile, second_tile)
    weight, slope_value = cutoff_switch(squared)
    weight = weight * pair_mask
    first_rho = first_tile[4] * first_tile[4]
    second_rho = second_tile[4] * second_tile[4]
    first_sum = lax.optimization_barrier(jnp.sum(weight * second_rho[None, :] / (squared + second_rho[None, :]), axis=1))
    second_sum = lax.optimization_barrier(jnp.sum(weight * first_rho[:, None] / (squared + first_rho[:, None]), axis=0))
    return (screen_factor * first_sum[None], screen_factor * second_sum[None])

def force_pair(first_tile, second_tile, pair_mask):
    displace, squared = separation(first_tile, second_tile)
    weight, slope_value = cutoff_switch(squared)
    radius_pair = first_tile[4][:, None] * second_tile[4][None, :]
    damping = jnp.exp(-squared / (4.0 * radius_pair))
    effective = jnp.sqrt(squared + radius_pair * damping)
    derivative = (1.0 - 0.25 * damping) / (2.0 * effective)
    charge_pair = first_tile[3][:, None] * second_tile[3][None, :]
    strength = 2.0 * coulomb_factor * charge_pair * pair_mask * (slope_value / effective - weight * derivative / (effective * effective))
    pushes = strength[None] * displace
    return (lax.optimization_barrier(jnp.sum(pushes, axis=2)), -lax.optimization_barrier(jnp.sum(pushes, axis=1)))

def pair_block(kernel, local_tiles, source_tiles, local_index, source_index, active):
    first_tiles = jnp.take(local_tiles, local_index, axis=1)
    second_tiles = jnp.take(source_tiles, source_index, axis=1)
    first_lane = lax.broadcasted_iota(jnp.int32, (128, 128), 0)
    second_lane = lax.broadcasted_iota(jnp.int32, (128, 128), 1)
    ordered = (first_lane < second_lane).astype(jnp.float32)
    diagonal = (local_index == source_index)[:, None, None]
    pair_mask = jnp.where(diagonal, ordered[None], 1.0) * active[:, None, None]
    return jax.vmap(kernel, in_axes=(1, 1, 0), out_axes=1)(first_tiles, second_tiles, pair_mask)

def brick_terms(kernel, out_rows, local_tiles, source_tiles, pair_list, live_count):
    tile_count = local_tiles.shape[1]

    def accumulate(totals, begin):
        local_index = lax.dynamic_slice_in_dim(pair_list[0], begin, 16)
        source_index = lax.dynamic_slice_in_dim(pair_list[1], begin, 16)
        active = (begin + jnp.arange(16, dtype=jnp.int32) < live_count).astype(jnp.float32)
        first_sum, second_sum = pair_block(kernel, local_tiles, source_tiles, local_index, source_index, active)
        return ((totals[0].at[:, local_index].add(first_sum), totals[1].at[:, source_index].add(second_sum)), None)
    empty = (jnp.zeros((out_rows, tile_count, 128), jnp.float32), jnp.zeros((out_rows, 5 * tile_count, 128), jnp.float32))
    totals, leftover = lax.scan(accumulate, empty, jnp.arange(0, pair_list.shape[1], 16, dtype=jnp.int32))
    return totals

def corner_offsets(rows):
    table = [[lengthwise * brick_side, across * brick_side] + [0.0] * (rows - 2) for lengthwise, across in half_shell]
    return jnp.array(table, jnp.float32)[:, :, None]

def neighbours(packed):
    stacked = jnp.stack([jnp.roll(packed, (-lengthwise, -across), axis=(0, 1)) for lengthwise, across in half_shell], axis=2)
    return stacked + corner_offsets(packed.shape[2])[None, None]

def all_bricks(kernel, out_rows, packed, ghosts, tile_pairs, tile_counts):
    wide_count, narrow_count, channels, atoms = packed.shape
    tile_count = atoms // 128
    bricks = wide_count * narrow_count
    local_tiles = packed.reshape(bricks, channels, tile_count, 128)
    source_tiles = jnp.transpose(ghosts, (0, 1, 3, 2, 4)).reshape(bricks, channels, 5 * tile_count, 128)
    pair_lists = tile_pairs.reshape(bricks, 2, tile_pairs.shape[-1])
    counts = tile_counts.reshape(bricks)

    def one_brick(brick_items):
        return brick_terms(kernel, out_rows, brick_items[0], brick_items[1], brick_items[2], brick_items[3])
    own_terms, returned = lax.map(one_brick, (local_tiles, source_tiles, pair_lists, counts))
    total = own_terms.reshape(wide_count, narrow_count, out_rows, atoms)
    returned = jnp.transpose(returned.reshape(wide_count, narrow_count, out_rows, 5, atoms), (0, 1, 3, 2, 4))
    for slot_index, (lengthwise, across) in enumerate(half_shell):
        total = total + jnp.roll(returned[:, :, slot_index], (lengthwise, across), axis=(0, 1))
    return total

def pack_migrants(atom_state, targets):
    headings = jnp.arange(1, 9, dtype=jnp.int32)
    matches = (targets[None, :] == headings[:, None]).astype(jnp.int32)
    ranks = jnp.cumsum(matches, axis=1).astype(jnp.int32) - 1
    block_base = MIGRANTS * jnp.arange(8, dtype=jnp.int32)[:, None]
    leaving = lax.optimization_barrier(jnp.sum(matches, axis=0)).astype(jnp.int32)
    landing = lax.optimization_barrier(jnp.sum(matches * (ranks + block_base), axis=0)).astype(jnp.int32)
    landing = jnp.where(leaving > 0, landing, 8 * MIGRANTS).astype(jnp.int32)
    rows = atom_state.shape[0]
    table = jnp.zeros((8 * MIGRANTS, rows), atom_state.dtype)
    table = table.at[landing].set(jnp.transpose(atom_state), mode='drop')
    return jnp.transpose(table.reshape(8, MIGRANTS, rows), (0, 2, 1))

def reference(positions, velocities, charges, radii, tile_pairs, tile_counts, destinations):
    coords = positions
    velocity = velocities
    shifts = []
    born_radius = radii
    for moment in range(STEPS):
        packed = jnp.concatenate([coords, charges[:, :, None], radii[:, :, None]], axis=2)
        screening = all_bricks(screen_pair, 1, packed, neighbours(packed), tile_pairs, tile_counts)[:, :, 0]
        born_radius = radii / (1.0 - 0.9 * jnp.tanh(screening))
        packed = jnp.concatenate([coords, charges[:, :, None], born_radius[:, :, None]], axis=2)
        forces = all_bricks(force_pair, 3, packed, neighbours(packed), tile_pairs, tile_counts)
        velocity = velocity + step_time * forces
        coords = coords + step_time * velocity
        moved = jnp.sqrt(lax.optimization_barrier(jnp.sum((coords - positions) ** 2, axis=2)))
        shifts.append(jnp.max(moved) / skin_depth)
    atom_state = jnp.concatenate([coords, velocity], axis=2)
    outgoing = jax.vmap(jax.vmap(pack_migrants))(atom_state, destinations)
    arrivals = jnp.stack([jnp.roll(outgoing[:, :, heading], neighbour_offsets[heading], axis=(0, 1)) for heading in range(8)], axis=2)
    return (coords, velocity, born_radius, arrivals, jnp.stack(shifts))
```

```python
import functools
import jax
import jax.numpy as jnp
from jax import lax
from jax.experimental import pallas as pl
from jax.experimental.pallas import tpu as pltpu
from jax.sharding import PartitionSpec as P

MIGRANTS = 64
STEPS = 3
WIDE = 32
NARROW = 8
AXES = ("wide", "narrow")

scale = 0.4
brick_side = 3.0
step_time = 0.1
skin_depth = 0.2
screen_factor = 0.3
log2e = 1.4426950408889634

ghost_offsets = (
    (0, 0), (0, -1), (0, 1), (-1, -1), (-1, 0), (-1, 1), (1, -1), (1, 0), (1, 1)
)
neighbour_offsets = ((-1, -1), (-1, 0), (-1, 1), (0, -1), (0, 1), (1, -1), (1, 0), (1, 1))
CHUNK = 16


def flat_device(x, y, z, core):
    return (y * 8 + (z // 4) * 4 + x) * 8 + (z % 4) * 2 + core


def ring_xz():
    ring = []
    for z in range(8):
        ring += [(x, z) for x in ((1, 2, 3) if z % 2 == 0 else (3, 2, 1))]
    return ring + [(0, z) for z in range(7, -1, -1)]


RING = ring_xz()


def home(w, n):
    return (w % WIDE) * NARROW + n % NARROW


def work(w, n):
    x, z = RING[w % WIDE]
    n = n % NARROW
    return flat_device(x, n if n < 4 else 7 - n, z, 0 if n < 4 else 1)


def send(shard, p=0, s=0, source=work, target=work):
    pairs = [
        (source(w, n), target(w + p, n + s)) for w in range(WIDE) for n in range(NARROW)
    ]
    return lax.ppermute(shard, AXES, pairs)


def device_of(index):
    w, n = divmod(index, NARROW)
    return (w % 4, w // 8, (w // 4) % 2 * 4 + n // 2, n % 2)


def everywhere_max(value):
    flips = ((0, 0, 0, 1), (1, 0, 0, 0), (2, 0, 0, 0), (0, 1, 0, 0), (0, 2, 0, 0),
             (0, 0, 1, 0), (0, 0, 2, 0), (0, 0, 4, 0))
    for flip in flips:
        pairs = []
        for index in range(WIDE * NARROW):
            place = device_of(index)
            pairs.append((index, flat_device(*(a ^ b for a, b in zip(place, flip)))))
        value = jnp.maximum(value, lax.ppermute(value, AXES, pairs))
    return value


def rank_rows(flags):
    rows = flags.shape[0]
    a = lax.broadcasted_iota(jnp.int32, (128, 128), 0)
    b = lax.broadcasted_iota(jnp.int32, (128, 128), 1)
    inside = jnp.dot(
        flags.astype(jnp.bfloat16), (a < b).astype(jnp.bfloat16),
        preferred_element_type=jnp.float32,
    )
    a = lax.broadcasted_iota(jnp.int32, (rows, rows), 0)
    b = lax.broadcasted_iota(jnp.int32, (rows, rows), 1)
    totals = jnp.sum(flags, axis=1, keepdims=True)
    before = jnp.dot(
        (b < a).astype(jnp.bfloat16), jnp.broadcast_to(totals, (rows, 128)).astype(jnp.bfloat16),
        preferred_element_type=jnp.float32,
    )
    return jnp.where(flags > 0, inside + before, -1.0), totals


def compact(candidates, capacity):
    flags = jnp.concatenate([c[0] for c in candidates], axis=0)
    first = jnp.concatenate([c[1] for c in candidates], axis=0)
    second = jnp.concatenate([c[2] for c in candidates], axis=0)
    ranks, totals = rank_rows(flags)
    slots = lax.broadcasted_iota(jnp.int32, (capacity, 128), 0).astype(jnp.float32)
    result = jnp.zeros((16, capacity), jnp.float32)
    for row in range(flags.shape[0]):
        hits = (slots == ranks[row:row + 1]).astype(jnp.bfloat16)
        values = jnp.concatenate(
            [jnp.broadcast_to(first[row:row + 1], (8, 128)),
             jnp.broadcast_to(second[row:row + 1], (8, 128))], axis=0
        ).astype(jnp.bfloat16)
        result = result + lax.dot_general(
            values, hits, (((1,), (1,)), ((), ())), preferred_element_type=jnp.float32
        )
    return (result[0:8] * 256.0 + result[8:16]).astype(jnp.int32), totals


def split_list(listed):
    local, source = listed[0:2], listed[2:4]
    slot = jnp.floor(source * (1.0 / 16.0))
    return local, slot, source - 16.0 * slot


def flag(condition):
    return jnp.where(condition, 1.0, 0.0)


def near_tasks(own_ref, behind_ref, tasks_ref, counts_ref):
    local, slot, tile = split_list(own_ref[...])
    inner = flag(slot == 0.0)
    diagonal = inner * flag(local == tile)
    plain = inner - diagonal
    b_local, b_slot, b_tile = split_list(behind_ref[...])
    tasks, totals = compact(
        [
            (diagonal, local, tile),
            (plain, local, tile),
            (plain, tile, local),
            (flag(slot == 4.0), local, 32.0 + tile),
            (flag(b_slot == 4.0), b_tile, 16.0 + b_local),
        ],
        NEAR_TASKS,
    )
    tasks_ref[...] = tasks
    lane = lax.broadcasted_iota(jnp.int32, (8, 128), 1)
    counts_ref[...] = jnp.where(
        lane == 0, jnp.sum(totals[0:2]), jnp.sum(totals)
    ).astype(jnp.int32)


def far_tasks(own_ref, behind_ref, tasks_ref, counts_ref):
    local, slot, tile = split_list(own_ref[...])
    ahead = flag(slot >= 1.0) * flag(slot <= 3.0)
    candidates = [(ahead, local, (5.0 + slot) * 16.0 + tile)]
    for brick, want in ((3, 3.0), (4, 2.0), (5, 1.0)):
        b_local, b_slot, b_tile = split_list(behind_ref[brick - 3])
        candidates.append((flag(b_slot == want), b_tile, 16.0 * brick + b_local))
    tasks, totals = compact(candidates, FAR_TASKS)
    tasks_ref[...] = tasks
    counts_ref[...] = jnp.broadcast_to(jnp.sum(totals), (8, 128)).astype(jnp.int32)


NEAR_TASKS = 640
FAR_TASKS = 1024


def make_tasks(kernel, capacity, own_list, behind_list):
    return pl.pallas_call(
        kernel,
        out_shape=(
            jax.ShapeDtypeStruct((8, capacity), jnp.int32),
            jax.ShapeDtypeStruct((8, 128), jnp.int32),
        ),
        compiler_params=pltpu.CompilerParams(vmem_limit_bytes=32 * 1024 * 1024),
    )(own_list, behind_list)


def fill_rows(target, bricks, offsets, component):
    for brick, (value, offset) in enumerate(zip(bricks, offsets)):
        shifted = value * scale
        if component < 2 and offset[component] != 0:
            shifted = (value + brick_side * offset[component]) * scale
        target[pl.ds(brick * 16, 16), :] = shifted


def expand(rows, targets):
    blank = jnp.zeros((128 - rows.shape[0], 128), jnp.float32)
    columns = jnp.transpose(jnp.concatenate([rows, blank], axis=0))
    for component, target in enumerate(targets):
        for tile in range(16):
            lane = component * 16 + tile
            target[tile] = jnp.broadcast_to(columns[:, lane:lane + 1], (128, 128))


def collapse(sources):
    lanes = lax.broadcasted_iota(jnp.int32, (128, 128), 1)
    result = jnp.zeros((128, 128), jnp.float32)
    for component, source in enumerate(sources):
        for tile in range(16):
            total = jnp.sum(source[tile], axis=1, keepdims=True)
            result = jnp.where(lanes == component * 16 + tile, total, result)
    return jnp.transpose(result)[0:16 * len(sources)]


def loop_tasks(tasks, low, high, step):
    def visit(k, carry):
        code = tasks[0, k]
        step(lax.shift_right_logical(code, 8), lax.bitwise_and(code, 255))
        return carry

    lax.fori_loop(low, high, visit, 0)


def not_self(begin):
    a = lax.broadcasted_iota(jnp.int32, (CHUNK, 128), 0) + begin
    b = lax.broadcasted_iota(jnp.int32, (CHUNK, 128), 1)
    return a != b


def screen_kernel(near, counts, tasks, own, radius, ghosts, ghost_radius, prior, out, scratch):
    gx, gy, gz, gr, ex, ey, ez, acc = scratch
    offsets = ghost_offsets[0:3] if near else ghost_offsets[3:9]
    for component, target in enumerate((gx, gy, gz)):
        rows = pl.ds(component * 16, 16)
        bricks = ([own[rows, :]] if near else []) + [ghost[rows, :] for ghost in ghosts]
        fill_rows(target, bricks, offsets, component)
    bricks = ([radius[...]] if near else []) + [ghost[...] for ghost in ghost_radius]
    for brick, value in enumerate(bricks):
        value = value * scale
        gr[pl.ds(brick * 16, 16), :] = value * value
    expand(own[...] * scale, (ex, ey, ez))
    acc[...] = jnp.zeros_like(acc)

    def step(masked, t, g):
        g = g if near else g - 48
        row = pl.ds(g, 1)
        bx, by, bz, br = gx[row, :], gy[row, :], gz[row, :], gr[row, :]
        for begin in range(0, 128, CHUNK):
            part = pl.ds(begin, CHUNK)
            dx = ex[t, part, :] - bx
            dy = ey[t, part, :] - by
            dz = ez[t, part, :] - bz
            u = dx * dx + dy * dy + dz * dz
            h = jnp.maximum(1.0 - u, 0.0)
            value = h * h * br * pl.reciprocal(u + br, approx=True)
            if masked:
                value = jnp.where(not_self(begin), value, 0.0)
            acc[t, part, :] += value

    if near:
        loop_tasks(tasks, 0, counts[0, 0], functools.partial(step, True))
        loop_tasks(tasks, counts[0, 0], counts[0, 1], functools.partial(step, False))
        out[...] = collapse((acc,))
    else:
        loop_tasks(tasks, 0, counts[0, 0], functools.partial(step, False))
        total = screen_factor * (collapse((acc,)) + prior[...])
        out[...] = radius[...] / (1.0 - 0.9 * jnp.tanh(total))


def force_kernel(near, counts, tasks, own, born, charge, ghosts, ghost_born, ghost_charge, extra,
                 outs, scratch):
    gx, gy, gz, gr, gk, gq, ex, ey, ez, er, ek, ax, ay, az = scratch
    offsets = ghost_offsets[0:3] if near else ghost_offsets[3:9]
    for component, target in enumerate((gx, gy, gz)):
        rows = pl.ds(component * 16, 16)
        bricks = ([own[rows, :]] if near else []) + [ghost[rows, :] for ghost in ghosts]
        fill_rows(target, bricks, offsets, component)
    bricks = ([born[...]] if near else []) + [ghost[...] for ghost in ghost_born]
    root = 1.25 * log2e ** 0.5
    for brick, value in enumerate(bricks):
        gr[pl.ds(brick * 16, 16), :] = value * scale
        gk[pl.ds(brick * 16, 16), :] = -root / value
    bricks = ([charge[...]] if near else []) + [ghost[...] for ghost in ghost_charge]
    for brick, value in enumerate(bricks):
        gq[pl.ds(brick * 16, 16), :] = value
    expand(
        jnp.concatenate([own[...] * scale, born[...] * scale, root / born[...]], axis=0),
        (ex, ey, ez, er, ek),
    )
    for acc in (ax, ay, az):
        acc[...] = jnp.zeros_like(acc)

    def step(masked, t, g):
        g = g if near else g - 48
        row = pl.ds(g, 1)
        bx, by, bz = gx[row, :], gy[row, :], gz[row, :]
        br, bk, bq = gr[row, :], gk[row, :], gq[row, :]
        for begin in range(0, 128, CHUNK):
            part = pl.ds(begin, CHUNK)
            dx = ex[t, part, :] - bx
            dy = ey[t, part, :] - by
            dz = ez[t, part, :] - bz
            u = dx * dx + dy * dy + dz * dz
            h = jnp.maximum(1.0 - u, 0.0)
            e = jnp.exp2(u * (ek[t, part, :] * bk))
            inverse = lax.rsqrt(u + er[t, part, :] * br * e)
            c = (bq * h) * inverse * (16.0 + h * (4.0 - e) * (inverse * inverse))
            if masked:
                c = jnp.where(not_self(begin), c, 0.0)
            ax[t, part, :] += c * dx
            ay[t, part, :] += c * dy
            az[t, part, :] += c * dz

    if near:
        loop_tasks(tasks, 0, counts[0, 0], functools.partial(step, True))
        loop_tasks(tasks, counts[0, 0], counts[0, 1], functools.partial(step, False))
        outs[0][...] = collapse((ax, ay, az))
    else:
        loop_tasks(tasks, 0, counts[0, 0], functools.partial(step, False))
        prior, velocity, anchor = extra
        total = collapse((ax, ay, az)) + prior[...]
        q = jnp.concatenate([charge[...]] * 3, axis=0)
        v = velocity[...] + step_time * (-0.02 * (q * total))
        x = own[...] + step_time * v
        moved = x - anchor[...]
        squared = moved * moved
        squared = squared[0:16] + squared[16:32] + squared[32:48]
        outs[0][...] = x
        outs[1][...] = v
        outs[2][...] = jnp.broadcast_to(jnp.max(jnp.sqrt(squared)), (8, 128))


def vmem(rows=None):
    return pl.BlockSpec(memory_space=pltpu.VMEM)


def smem():
    return pl.BlockSpec(memory_space=pltpu.SMEM)


def params():
    return pltpu.CompilerParams(vmem_limit_bytes=40 * 1024 * 1024)


def tile_scratch(count):
    return [pltpu.VMEM((16, 128, 128), jnp.float32) for _ in range(count)]


def row_scratch(count, bricks):
    return [pltpu.VMEM((bricks * 16, 128), jnp.float32) for _ in range(count)]


def cost(flops):
    return pl.CostEstimate(flops=flops, bytes_accessed=1 << 20, transcendentals=flops // 16)


def screen(near, counts, tasks, own, radius, ghosts, ghost_radius, prior=None):
    many = len(ghosts)
    extra = [] if near else [prior]

    def kernel(*refs):
        counts, tasks, own, radius = refs[0:4]
        ghosts, ghost_radius = refs[4:4 + many], refs[4 + many:4 + 2 * many]
        rest = refs[4 + 2 * many:]
        prior, rest = (None, rest) if near else (rest[0], rest[1:])
        screen_kernel(near, counts, tasks, own, radius, ghosts, ghost_radius, prior, rest[0],
                      rest[1:])

    bricks = 3 if near else 6
    return pl.pallas_call(
        kernel,
        out_shape=jax.ShapeDtypeStruct((16, 128), jnp.float32),
        in_specs=[smem(), smem()] + [vmem()] * (2 + 2 * many + len(extra)),
        out_specs=vmem(),
        scratch_shapes=row_scratch(4, bricks) + tile_scratch(4),
        compiler_params=params(),
        cost_estimate=cost(1 << 26),
    )(counts, tasks, own, radius, *ghosts, *ghost_radius, *extra)


def force(near, counts, tasks, own, born, charge, ghosts, ghost_born, ghost_charge, extra=()):
    many = len(ghosts)

    def kernel(*refs):
        counts, tasks, own, born, charge = refs[0:5]
        rest = refs[5:]
        ghosts, ghost_born, ghost_charge = (
            rest[0:many], rest[many:2 * many], rest[2 * many:3 * many]
        )
        rest = rest[3 * many:]
        extras, rest = rest[0:len(extra)], rest[len(extra):]
        outs = 1 if near else 3
        force_kernel(near, counts, tasks, own, born, charge, ghosts, ghost_born, ghost_charge,
                     extras, rest[0:outs], rest[outs:])

    bricks = 3 if near else 6
    rows = jax.ShapeDtypeStruct((48, 128), jnp.float32)
    out_shape = (rows,) if near else (rows, rows, jax.ShapeDtypeStruct((8, 128), jnp.float32))
    return pl.pallas_call(
        kernel,
        out_shape=out_shape,
        in_specs=[smem(), smem()] + [vmem()] * (3 + 3 * many + len(extra)),
        out_specs=tuple(vmem() for _ in out_shape),
        scratch_shapes=row_scratch(6, bricks) + tile_scratch(8),
        compiler_params=params(),
        cost_estimate=cost(1 << 27),
    )(counts, tasks, own, born, charge, *ghosts, *ghost_born, *ghost_charge, *extra)


def slots_kernel(targets, out):
    codes = targets[...]
    result = jnp.full((16, 128), -1.0, jnp.float32)
    for heading in range(1, 9):
        flags = flag(codes == float(heading))
        ranks, totals = rank_rows(flags)
        result = jnp.where(flags > 0, ranks + float(MIGRANTS * (heading - 1)), result)
    out[...] = result


def migrant_slots(targets):
    return pl.pallas_call(
        slots_kernel, out_shape=jax.ShapeDtypeStruct((16, 128), jnp.float32)
    )(targets)


def pack_kernel(slots, position, velocity, out):
    def parts(value):
        high = value.astype(jnp.bfloat16)
        left = value - high.astype(jnp.float32)
        middle = left.astype(jnp.bfloat16)
        low = (left - middle.astype(jnp.float32)).astype(jnp.bfloat16)
        return high.astype(jnp.float32), middle.astype(jnp.float32), low.astype(jnp.float32)

    split = parts(position[...]), parts(velocity[...])
    wanted = lax.broadcasted_iota(jnp.int32, (8 * MIGRANTS, 128), 0).astype(jnp.float32)
    result = jnp.zeros((32, 8 * MIGRANTS), jnp.float32)
    blank = jnp.zeros((2, 128), jnp.float32)
    for tile in range(16):
        hits = (wanted == slots[tile:tile + 1, :]).astype(jnp.bfloat16)
        rows = []
        for piece in range(3):
            for kind in range(2):
                for component in range(3):
                    row = component * 16 + tile
                    rows.append(split[kind][piece][row:row + 1])
            rows.append(blank)
        rows.append(jnp.zeros((8, 128), jnp.float32))
        state = jnp.concatenate(rows, axis=0).astype(jnp.bfloat16)
        result = result + lax.dot_general(
            state, hits, (((1,), (1,)), ((), ())), preferred_element_type=jnp.float32
        )
    out[...] = (result[0:8] + result[8:16]) + result[16:24]


def pack_migrants(slots, position, velocity):
    table = pl.pallas_call(
        pack_kernel,
        out_shape=jax.ShapeDtypeStruct((8, 8 * MIGRANTS), jnp.float32),
        compiler_params=params(),
    )(slots, position, velocity)
    return jnp.transpose(table[0:6].reshape(6, 8, MIGRANTS), (1, 0, 2))


def across(value):
    return send(value, 0, 1), send(value, 0, -1)


def along(value):
    return send(value, 1, 0), send(value, -1, 0)


def body(positions, velocities, charges, radii, tile_pairs, tile_counts, destinations):
    live = jnp.arange(tile_pairs.shape[3], dtype=jnp.int32) < tile_counts[0, 0]
    listed = jnp.where(live[None], tile_pairs[0, 0], -1).astype(jnp.float32).reshape(4, 128)
    first = jnp.concatenate(
        [
            positions.reshape(48, 128),
            charges.reshape(16, 128),
            radii.reshape(16, 128),
            listed,
            jnp.zeros((4, 128), jnp.float32),
        ]
    )
    later = jnp.concatenate(
        [velocities.reshape(48, 128), destinations.reshape(16, 128).astype(jnp.float32)]
    )
    first = send(first, source=home)
    later = send(later, source=home)
    coords = anchor = first[0:48]
    charge, radius, own_list = first[48:64], first[64:80], first[80:84]
    velocity = later[0:48]
    slots = migrant_slots(later[48:64])

    shifts = []
    for moment in range(STEPS):
        message = first if moment == 0 else coords
        lower, upper = across(message)
        row = jnp.stack([lower, message, upper])
        behind, ahead = along(row)
        if moment == 0:
            near_charge = (lower[48:64], upper[48:64])
            near_radius = (lower[64:80], upper[64:80])
            near_list = make_tasks(near_tasks, NEAR_TASKS, own_list, lower[80:84])
            far_charge = tuple(block[k, 48:64] for block in (behind, ahead) for k in range(3))
            far_radius = tuple(block[k, 64:80] for block in (behind, ahead) for k in range(3))
            far_list = make_tasks(far_tasks, FAR_TASKS, own_list, behind[:, 80:84])
            near_list = (near_list[1], near_list[0])
            far_list = (far_list[1], far_list[0])
        near = (lower[0:48], upper[0:48])
        far = tuple(block[k, 0:48] for block in (behind, ahead) for k in range(3))
        partial = screen(True, *near_list, coords, radius, near, near_radius)
        born = screen(False, *far_list, coords, radius, far, far_radius, partial)
        born_lower, born_upper = across(born)
        row = jnp.stack([born_lower, born, born_upper])
        behind, ahead = along(row)
        far_born = tuple(block[k] for block in (behind, ahead) for k in range(3))
        (partial,) = force(
            True, *near_list, coords, born, charge, near, (born_lower, born_upper), near_charge
        )
        coords, velocity, moved = force(
            False, *far_list, coords, born, charge, far, far_born, far_charge,
            (partial, velocity, anchor),
        )
        shifts.append(moved[0:1])

    shift = everywhere_max(jnp.concatenate(shifts, axis=0))[:, 0] / skin_depth
    outgoing = pack_migrants(slots, coords, velocity)
    back, forth = send(outgoing[0:3], -1, 0), send(outgoing[5:8], 1, 0)
    arrived_lower = jnp.stack([back[0], outgoing[3], forth[0]])
    arrived_upper = jnp.stack([back[2], outgoing[4], forth[2]])
    down = send(arrived_lower, 0, -1, target=home)
    up = send(arrived_upper, 0, 1, target=home)
    rest = jnp.concatenate(
        [coords, velocity, born, back[1].reshape(3, 128), forth[1].reshape(3, 128)]
    )
    rest = send(rest, target=home)
    straight = rest[112:118].reshape(2, 6, MIGRANTS)
    arrivals = jnp.stack(
        [down[0], straight[0], up[0], down[1], up[1], down[2], straight[1], up[2]]
    )
    return (
        rest[0:48].reshape(1, 1, 3, 2048),
        rest[48:96].reshape(1, 1, 3, 2048),
        rest[96:112].reshape(1, 1, 2048),
        arrivals[None, None],
        shift,
    )


def solution(mesh):
    in_specs = (
        P("wide", "narrow", None, None),
        P("wide", "narrow", None, None),
        P("wide", "narrow", None),
        P("wide", "narrow", None),
        P("wide", "narrow", None, None),
        P("wide", "narrow"),
        P("wide", "narrow", None),
    )
    out_specs = (
        P("wide", "narrow", None, None),
        P("wide", "narrow", None, None),
        P("wide", "narrow", None),
        P("wide", "narrow", None, None, None),
        P(),
    )
    return jax.shard_map(body, mesh=mesh, in_specs=in_specs, out_specs=out_specs, check_vma=False)
```

```python
import functools
import jax
import jax.numpy as jnp
from jax import lax
from jax.experimental import pallas as pl
from jax.experimental.pallas import tpu as pltpu
from jax.sharding import PartitionSpec as P

MIGRANTS = 64
STEPS = 3
WIDE = 32
NARROW = 8
AXES = ("wide", "narrow")

scale = 0.4
brick_side = 3.0
step_time = 0.1
skin_depth = 0.2
screen_factor = 0.3
log2e = 1.4426950408889634

ghost_offsets = (
    (0, 0), (0, -1), (0, 1), (-1, -1), (-1, 0), (-1, 1), (1, -1), (1, 0), (1, 1)
)
neighbour_offsets = ((-1, -1), (-1, 0), (-1, 1), (0, -1), (0, 1), (1, -1), (1, 0), (1, 1))
CHUNK = 16
BATCH = 8


def flat_device(x, y, z, core):
    return (y * 8 + (z // 4) * 4 + x) * 8 + (z % 4) * 2 + core


def ring_xz():
    ring = []
    for z in range(8):
        ring += [(x, z) for x in ((1, 2, 3) if z % 2 == 0 else (3, 2, 1))]
    return ring + [(0, z) for z in range(7, -1, -1)]


RING = ring_xz()


def home(w, n):
    return (w % WIDE) * NARROW + n % NARROW


def work(w, n):
    x, z = RING[w % WIDE]
    n = n % NARROW
    return flat_device(x, n if n < 4 else 7 - n, z, 0 if n < 4 else 1)


def send(shard, p=0, s=0, source=work, target=work):
    pairs = [
        (source(w, n), target(w + p, n + s)) for w in range(WIDE) for n in range(NARROW)
    ]
    return lax.ppermute(shard, AXES, pairs)


def device_of(index):
    w, n = divmod(index, NARROW)
    return (w % 4, w // 8, (w // 4) % 2 * 4 + n // 2, n % 2)


def flip_max(value, *flips):
    for flip in flips:
        pairs = []
        for index in range(WIDE * NARROW):
            place = device_of(index)
            pairs.append((index, flat_device(*(a ^ b for a, b in zip(place, flip)))))
        value = jnp.maximum(value, lax.ppermute(value, AXES, pairs))
    return value


def rank_rows(flags):
    rows = flags.shape[0]
    a = lax.broadcasted_iota(jnp.int32, (128, 128), 0)
    b = lax.broadcasted_iota(jnp.int32, (128, 128), 1)
    inside = jnp.dot(
        flags.astype(jnp.bfloat16), (a < b).astype(jnp.bfloat16),
        preferred_element_type=jnp.float32,
    )
    a = lax.broadcasted_iota(jnp.int32, (rows, rows), 0)
    b = lax.broadcasted_iota(jnp.int32, (rows, rows), 1)
    totals = jnp.sum(flags, axis=1, keepdims=True)
    before = jnp.dot(
        (b < a).astype(jnp.bfloat16), jnp.broadcast_to(totals, (rows, 128)).astype(jnp.bfloat16),
        preferred_element_type=jnp.float32,
    )
    return jnp.where(flags > 0, inside + before, -1.0), totals


def compact(candidates, capacity, spare):
    flags = jnp.concatenate([c[0] for c in candidates], axis=0)
    first = jnp.concatenate([c[1] for c in candidates], axis=0)
    second = jnp.concatenate([c[2] for c in candidates], axis=0)
    ranks, totals = rank_rows(flags)
    slots = lax.broadcasted_iota(jnp.int32, (capacity, 128), 0).astype(jnp.float32)
    result = jnp.zeros((16, capacity), jnp.float32)
    for row in range(flags.shape[0]):
        hits = (slots == ranks[row:row + 1]).astype(jnp.bfloat16)
        values = jnp.concatenate(
            [jnp.broadcast_to(first[row:row + 1], (8, 128)),
             jnp.broadcast_to(second[row:row + 1], (8, 128))], axis=0
        ).astype(jnp.bfloat16)
        result = result + lax.dot_general(
            values, hits, (((1,), (1,)), ((), ())), preferred_element_type=jnp.float32
        )
    index = lax.broadcasted_iota(jnp.int32, (8, capacity), 1)
    codes = (result[0:8] * 256.0 + result[8:16]).astype(jnp.int32)
    count = jnp.sum(totals)
    return jnp.where(index < count.astype(jnp.int32), codes, 16 * 256 + spare)[0:1], count


def split_list(listed):
    local, source = listed[0:2], listed[2:4]
    slot = jnp.floor(source * (1.0 / 16.0))
    return local, slot, source - 16.0 * slot


def flag(condition):
    return jnp.where(condition, 1.0, 0.0)


def near_tasks(own_ref, behind_ref, tasks_ref, counts_ref):
    local, slot, tile = split_list(own_ref[...])
    inner = flag(slot == 0.0)
    diagonal = inner * flag(local == tile)
    b_local, b_slot, b_tile = split_list(behind_ref[...])
    plain_tasks, plain = compact(
        [
            (inner - diagonal, local, tile),
            (inner - diagonal, tile, local),
            (flag(slot == 4.0), local, 32.0 + tile),
            (flag(b_slot == 4.0), b_tile, 16.0 + b_local),
        ],
        NEAR_TASKS, 0,
    )
    self_tasks, selves = compact([(diagonal, local, tile)], 128, 0)
    tasks_ref[...] = jnp.concatenate([plain_tasks, self_tasks], axis=1)
    lane = lax.broadcasted_iota(jnp.int32, (8, 128), 1)
    counts_ref[...] = jnp.where(lane == 0, plain, selves).astype(jnp.int32)


def far_tasks(own_ref, behind_ref, tasks_ref, counts_ref):
    local, slot, tile = split_list(own_ref[...])
    ahead = flag(slot >= 1.0) * flag(slot <= 3.0)
    candidates = [(ahead, local, (5.0 + slot) * 16.0 + tile)]
    for brick, want in ((3, 3.0), (4, 2.0), (5, 1.0)):
        b_local, b_slot, b_tile = split_list(behind_ref[brick - 3])
        candidates.append((flag(b_slot == want), b_tile, 16.0 * brick + b_local))
    tasks, count = compact(candidates, FAR_TASKS, 48)
    tasks_ref[...] = tasks
    counts_ref[...] = jnp.broadcast_to(count, (8, 128)).astype(jnp.int32)


NEAR_TASKS = 640
FAR_TASKS = 1152


def make_tasks(kernel, capacity, own_list, behind_list):
    return pl.pallas_call(
        kernel,
        out_shape=(
            jax.ShapeDtypeStruct((1, capacity), jnp.int32),
            jax.ShapeDtypeStruct((8, 128), jnp.int32),
        ),
        compiler_params=pltpu.CompilerParams(vmem_limit_bytes=32 * 1024 * 1024),
    )(own_list, behind_list)


def fill_rows(target, bricks, offsets, component):
    for brick, (value, offset) in enumerate(zip(bricks, offsets)):
        shifted = value * scale
        if component < 2 and offset[component] != 0:
            shifted = (value + brick_side * offset[component]) * scale
        target[pl.ds(brick * 16, 16), :] = shifted


def expand(rows, targets):
    blank = jnp.zeros((128 - rows.shape[0], 128), jnp.float32)
    columns = jnp.transpose(jnp.concatenate([rows, blank], axis=0))
    for component, target in enumerate(targets):
        for tile in range(16):
            lane = component * 16 + tile
            target[tile] = jnp.broadcast_to(columns[:, lane:lane + 1], (128, 128))
        target[16] = jnp.ones((128, 128), jnp.float32)


def collapse(sources):
    lanes = lax.broadcasted_iota(jnp.int32, (128, 128), 1)
    result = jnp.zeros((128, 128), jnp.float32)
    for component, source in enumerate(sources):
        for tile in range(16):
            total = jnp.sum(source[tile], axis=1, keepdims=True)
            result = jnp.where(lanes == component * 16 + tile, total, result)
    return jnp.transpose(result)[0:16 * len(sources)]


def loop_tasks(tasks, count, step):
    def visit(turn, carry):
        for lane in range(BATCH):
            code = tasks[0, turn * BATCH + lane]
            step(lax.shift_right_logical(code, 8), lax.bitwise_and(code, 255))
        return carry

    lax.fori_loop(0, lax.div(count + (BATCH - 1), BATCH), visit, 0)


def loop_single(tasks, begin, count, step):
    def visit(k, carry):
        code = tasks[0, begin + k]
        step(lax.shift_right_logical(code, 8), lax.bitwise_and(code, 255))
        return carry

    lax.fori_loop(0, count, visit, 0)


def not_self(begin):
    a = lax.broadcasted_iota(jnp.int32, (CHUNK, 128), 0) + begin
    b = lax.broadcasted_iota(jnp.int32, (CHUNK, 128), 1)
    return a != b


def screen_kernel(near, counts, tasks, own, radius, ghosts, ghost_radius, prior, out, scratch):
    gx, gy, gz, gr, ex, ey, ez, acc = scratch
    offsets = ghost_offsets[0:3] if near else ghost_offsets[3:9]
    for component, target in enumerate((gx, gy, gz)):
        rows = pl.ds(component * 16, 16)
        bricks = ([own[rows, :]] if near else []) + [ghost[rows, :] for ghost in ghosts]
        fill_rows(target, bricks, offsets, component)
    bricks = ([radius[...]] if near else []) + [ghost[...] for ghost in ghost_radius]
    for brick, value in enumerate(bricks):
        value = value * scale
        gr[pl.ds(brick * 16, 16), :] = value * value
    expand(own[...] * scale, (ex, ey, ez))
    acc[...] = jnp.zeros_like(acc)

    def step(masked, t, g):
        g = g if near else g - 48
        row = pl.ds(g, 1)
        bx, by, bz, br = gx[row, :], gy[row, :], gz[row, :], gr[row, :]
        for begin in range(0, 128, CHUNK):
            part = pl.ds(begin, CHUNK)
            dx = ex[t, part, :] - bx
            dy = ey[t, part, :] - by
            dz = ez[t, part, :] - bz
            u = dx * dx + dy * dy + dz * dz
            h = jnp.maximum(1.0 - u, 0.0)
            value = h * h * br * pl.reciprocal(u + br, approx=True)
            if masked:
                value = jnp.where(not_self(begin), value, 0.0)
            acc[t, part, :] += value

    if near:
        loop_single(tasks, NEAR_TASKS, counts[0, 1], functools.partial(step, True))
        loop_tasks(tasks, counts[0, 0], functools.partial(step, False))
        out[...] = collapse((acc,))
    else:
        loop_tasks(tasks, counts[0, 0], functools.partial(step, False))
        total = screen_factor * (collapse((acc,)) + prior[...])
        out[...] = radius[...] / (1.0 - 0.9 * jnp.tanh(total))


def force_kernel(near, counts, tasks, own, born, charge, ghosts, ghost_born, ghost_charge, extra,
                 outs, scratch):
    gx, gy, gz, gr, gk, gq, ex, ey, ez, er, ek, ax, ay, az = scratch
    offsets = ghost_offsets[0:3] if near else ghost_offsets[3:9]
    for component, target in enumerate((gx, gy, gz)):
        rows = pl.ds(component * 16, 16)
        bricks = ([own[rows, :]] if near else []) + [ghost[rows, :] for ghost in ghosts]
        fill_rows(target, bricks, offsets, component)
    bricks = ([born[...]] if near else []) + [ghost[...] for ghost in ghost_born]
    root = 1.25 * log2e ** 0.5
    for brick, value in enumerate(bricks):
        gr[pl.ds(brick * 16, 16), :] = value * scale
        gk[pl.ds(brick * 16, 16), :] = -root / value
    bricks = ([charge[...]] if near else []) + [ghost[...] for ghost in ghost_charge]
    for brick, value in enumerate(bricks):
        gq[pl.ds(brick * 16, 16), :] = value
    expand(
        jnp.concatenate([own[...] * scale, born[...] * scale, root / born[...]], axis=0),
        (ex, ey, ez, er, ek),
    )
    for acc in (ax, ay, az):
        acc[...] = jnp.zeros_like(acc)

    def step(masked, t, g):
        g = g if near else g - 48
        row = pl.ds(g, 1)
        bx, by, bz = gx[row, :], gy[row, :], gz[row, :]
        br, bk, bq = gr[row, :], gk[row, :], gq[row, :]
        for begin in range(0, 128, CHUNK):
            part = pl.ds(begin, CHUNK)
            dx = ex[t, part, :] - bx
            dy = ey[t, part, :] - by
            dz = ez[t, part, :] - bz
            u = dx * dx + dy * dy + dz * dz
            h = jnp.maximum(1.0 - u, 0.0)
            e = jnp.exp2(u * (ek[t, part, :] * bk))
            inverse = lax.rsqrt(u + er[t, part, :] * br * e)
            w = h * inverse
            c = (bq * w) * (16.0 + (4.0 - e) * (w * inverse))
            if masked:
                c = jnp.where(not_self(begin), c, 0.0)
            ax[t, part, :] += c * dx
            ay[t, part, :] += c * dy
            az[t, part, :] += c * dz

    if near:
        loop_single(tasks, NEAR_TASKS, counts[0, 1], functools.partial(step, True))
        loop_tasks(tasks, counts[0, 0], functools.partial(step, False))
        outs[0][...] = collapse((ax, ay, az))
    else:
        loop_tasks(tasks, counts[0, 0], functools.partial(step, False))
        prior, velocity, anchor = extra
        total = collapse((ax, ay, az)) + prior[...]
        q = jnp.concatenate([charge[...]] * 3, axis=0)
        v = velocity[...] + step_time * (-0.02 * (q * total))
        x = own[...] + step_time * v
        moved = x - anchor[...]
        squared = moved * moved
        squared = squared[0:16] + squared[16:32] + squared[32:48]
        outs[0][...] = x
        outs[1][...] = v
        outs[2][...] = jnp.broadcast_to(jnp.max(jnp.sqrt(squared)), (8, 128))


def vmem(rows=None):
    return pl.BlockSpec(memory_space=pltpu.VMEM)


def smem():
    return pl.BlockSpec(memory_space=pltpu.SMEM)


def params():
    return pltpu.CompilerParams(vmem_limit_bytes=40 * 1024 * 1024)


def tile_scratch(count):
    return [pltpu.VMEM((17, 128, 128), jnp.float32) for _ in range(count)]


def row_scratch(count, bricks):
    return [pltpu.VMEM((bricks * 16, 128), jnp.float32) for _ in range(count)]


def cost(flops):
    return pl.CostEstimate(flops=flops, bytes_accessed=1 << 20, transcendentals=flops // 16)


def screen(near, counts, tasks, own, radius, ghosts, ghost_radius, prior=None):
    many = len(ghosts)
    extra = [] if near else [prior]

    def kernel(*refs):
        counts, tasks, own, radius = refs[0:4]
        ghosts, ghost_radius = refs[4:4 + many], refs[4 + many:4 + 2 * many]
        rest = refs[4 + 2 * many:]
        prior, rest = (None, rest) if near else (rest[0], rest[1:])
        screen_kernel(near, counts, tasks, own, radius, ghosts, ghost_radius, prior, rest[0],
                      rest[1:])

    bricks = 3 if near else 6
    return pl.pallas_call(
        kernel,
        out_shape=jax.ShapeDtypeStruct((16, 128), jnp.float32),
        in_specs=[smem(), smem()] + [vmem()] * (2 + 2 * many + len(extra)),
        out_specs=vmem(),
        scratch_shapes=row_scratch(4, bricks) + tile_scratch(4),
        compiler_params=params(),
        cost_estimate=cost(1 << 26),
    )(counts, tasks, own, radius, *ghosts, *ghost_radius, *extra)


def force(near, counts, tasks, own, born, charge, ghosts, ghost_born, ghost_charge, extra=()):
    many = len(ghosts)

    def kernel(*refs):
        counts, tasks, own, born, charge = refs[0:5]
        rest = refs[5:]
        ghosts, ghost_born, ghost_charge = (
            rest[0:many], rest[many:2 * many], rest[2 * many:3 * many]
        )
        rest = rest[3 * many:]
        extras, rest = rest[0:len(extra)], rest[len(extra):]
        outs = 1 if near else 3
        force_kernel(near, counts, tasks, own, born, charge, ghosts, ghost_born, ghost_charge,
                     extras, rest[0:outs], rest[outs:])

    bricks = 3 if near else 6
    rows = jax.ShapeDtypeStruct((48, 128), jnp.float32)
    out_shape = (rows,) if near else (rows, rows, jax.ShapeDtypeStruct((8, 128), jnp.float32))
    return pl.pallas_call(
        kernel,
        out_shape=out_shape,
        in_specs=[smem(), smem()] + [vmem()] * (3 + 3 * many + len(extra)),
        out_specs=tuple(vmem() for _ in out_shape),
        scratch_shapes=row_scratch(6, bricks) + tile_scratch(8),
        compiler_params=params(),
        cost_estimate=cost(1 << 27),
    )(counts, tasks, own, born, charge, *ghosts, *ghost_born, *ghost_charge, *extra)


def slots_kernel(targets, out):
    codes = targets[...]
    result = jnp.full((16, 128), -1.0, jnp.float32)
    for heading in range(1, 9):
        flags = flag(codes == float(heading))
        ranks, totals = rank_rows(flags)
        result = jnp.where(flags > 0, ranks + float(MIGRANTS * (heading - 1)), result)
    out[...] = result


def migrant_slots(targets):
    return pl.pallas_call(
        slots_kernel, out_shape=jax.ShapeDtypeStruct((16, 128), jnp.float32)
    )(targets)


def pack_kernel(slots, position, velocity, out):
    def parts(value):
        high = value.astype(jnp.bfloat16)
        left = value - high.astype(jnp.float32)
        middle = left.astype(jnp.bfloat16)
        low = (left - middle.astype(jnp.float32)).astype(jnp.bfloat16)
        return high.astype(jnp.float32), middle.astype(jnp.float32), low.astype(jnp.float32)

    split = parts(position[...]), parts(velocity[...])
    wanted = lax.broadcasted_iota(jnp.int32, (8 * MIGRANTS, 128), 0).astype(jnp.float32)
    result = jnp.zeros((32, 8 * MIGRANTS), jnp.float32)
    blank = jnp.zeros((2, 128), jnp.float32)
    for tile in range(16):
        hits = (wanted == slots[tile:tile + 1, :]).astype(jnp.bfloat16)
        rows = []
        for piece in range(3):
            for kind in range(2):
                for component in range(3):
                    row = component * 16 + tile
                    rows.append(split[kind][piece][row:row + 1])
            rows.append(blank)
        rows.append(jnp.zeros((8, 128), jnp.float32))
        state = jnp.concatenate(rows, axis=0).astype(jnp.bfloat16)
        result = result + lax.dot_general(
            state, hits, (((1,), (1,)), ((), ())), preferred_element_type=jnp.float32
        )
    out[...] = (result[0:8] + result[8:16]) + result[16:24]


def pack_migrants(slots, position, velocity):
    table = pl.pallas_call(
        pack_kernel,
        out_shape=jax.ShapeDtypeStruct((8, 8 * MIGRANTS), jnp.float32),
        compiler_params=params(),
    )(slots, position, velocity)
    return jnp.transpose(table[0:6].reshape(6, 8, MIGRANTS), (1, 0, 2))


def across(value):
    return send(value, 0, 1), send(value, 0, -1)


def along(value):
    return send(value, 1, 0), send(value, -1, 0)


def body(positions, velocities, charges, radii, tile_pairs, tile_counts, destinations):
    live = jnp.arange(tile_pairs.shape[3], dtype=jnp.int32) < tile_counts[0, 0]
    listed = jnp.where(live[None], tile_pairs[0, 0], -1).astype(jnp.float32).reshape(4, 128)
    first = jnp.concatenate(
        [
            positions.reshape(48, 128),
            charges.reshape(16, 128),
            radii.reshape(16, 128),
            listed,
            jnp.zeros((4, 128), jnp.float32),
        ]
    )
    later = jnp.concatenate(
        [velocities.reshape(48, 128), destinations.reshape(16, 128).astype(jnp.float32)]
    )
    first = send(first, source=home)
    later = send(later, source=home)
    coords = anchor = first[0:48]
    charge, radius, own_list = first[48:64], first[64:80], first[80:84]
    velocity = later[0:48]
    slots = migrant_slots(later[48:64])

    shifts = []
    for moment in range(STEPS):
        message = first if moment == 0 else coords
        lower, upper = across(message)
        row = jnp.stack([lower, message, upper])
        behind, ahead = along(row)
        if moment == 0:
            near_charge = (lower[48:64], upper[48:64])
            near_radius = (lower[64:80], upper[64:80])
            near_list = make_tasks(near_tasks, NEAR_TASKS + 128, own_list, lower[80:84])
            far_charge = tuple(block[k, 48:64] for block in (behind, ahead) for k in range(3))
            far_radius = tuple(block[k, 64:80] for block in (behind, ahead) for k in range(3))
            far_list = make_tasks(far_tasks, FAR_TASKS, own_list, behind[:, 80:84])
            near_list = (near_list[1], near_list[0])
            far_list = (far_list[1], far_list[0])
        near = (lower[0:48], upper[0:48])
        far = tuple(block[k, 0:48] for block in (behind, ahead) for k in range(3))
        partial = screen(True, *near_list, coords, radius, near, near_radius)
        born = screen(False, *far_list, coords, radius, far, far_radius, partial)
        born_lower, born_upper = across(born)
        row = jnp.stack([born_lower, born, born_upper])
        behind, ahead = along(row)
        far_born = tuple(block[k] for block in (behind, ahead) for k in range(3))
        (partial,) = force(
            True, *near_list, coords, born, charge, near, (born_lower, born_upper), near_charge
        )
        coords, velocity, moved = force(
            False, *far_list, coords, born, charge, far, far_born, far_charge,
            (partial, velocity, anchor),
        )
        shifts.append(moved[0:1])
        if moment == 0:
            slots, velocity = lax.optimization_barrier((slots, velocity))

    outgoing = pack_migrants(slots, coords, velocity)
    shift = jnp.concatenate(shifts, axis=0)
    outgoing, shift = lax.optimization_barrier((outgoing, shift))
    back, forth = send(outgoing[0:3], -1, 0), send(outgoing[5:8], 1, 0)
    shift = flip_max(shift, (0, 0, 0, 1))
    back, forth, shift = lax.optimization_barrier((back, forth, shift))
    down = send(jnp.stack([back[0], outgoing[3], forth[0]]), 0, -1)
    up = send(jnp.stack([back[2], outgoing[4], forth[2]]), 0, 1)
    shift = flip_max(shift, (1, 0, 0, 0))
    down, up, shift = lax.optimization_barrier((down, up, shift))
    arrivals = jnp.stack([down[0], back[1], up[0], down[1], up[1], down[2], forth[1], up[2]])
    rest = jnp.concatenate([coords, velocity, born, arrivals.reshape(24, 128)])
    rest = send(rest, target=home)
    shift = flip_max(shift, (2, 0, 0, 0), (0, 1, 0, 0), (0, 2, 0, 0))
    rest, shift = lax.optimization_barrier((rest, shift))
    shift = flip_max(shift, (0, 0, 1, 0), (0, 0, 2, 0), (0, 0, 4, 0))
    shift = shift[:, 0] / skin_depth
    arrivals = rest[112:136].reshape(8, 6, MIGRANTS)
    return (
        rest[0:48].reshape(1, 1, 3, 2048),
        rest[48:96].reshape(1, 1, 3, 2048),
        rest[96:112].reshape(1, 1, 2048),
        arrivals[None, None],
        shift,
    )


def solution(mesh):
    in_specs = (
        P("wide", "narrow", None, None),
        P("wide", "narrow", None, None),
        P("wide", "narrow", None),
        P("wide", "narrow", None),
        P("wide", "narrow", None, None),
        P("wide", "narrow"),
        P("wide", "narrow", None),
    )
    out_specs = (
        P("wide", "narrow", None, None),
        P("wide", "narrow", None, None),
        P("wide", "narrow", None),
        P("wide", "narrow", None, None, None),
        P(),
    )
    return jax.shard_map(body, mesh=mesh, in_specs=in_specs, out_specs=out_specs, check_vma=False)
```

```python
import functools
import jax
import jax.numpy as jnp
from jax import lax
from jax.experimental import pallas as pl
from jax.experimental.pallas import tpu as pltpu
from jax.sharding import PartitionSpec as P

MIGRANTS = 64
STEPS = 3
WIDE = 32
NARROW = 8
AXES = ("wide", "narrow")

scale = 0.4
brick_side = 3.0
step_time = 0.1
skin_depth = 0.2
screen_factor = 0.3
log2e = 1.4426950408889634

ghost_offsets = (
    (0, 0), (0, -1), (0, 1), (-1, -1), (-1, 0), (-1, 1), (1, -1), (1, 0), (1, 1)
)
neighbour_offsets = ((-1, -1), (-1, 0), (-1, 1), (0, -1), (0, 1), (1, -1), (1, 0), (1, 1))
CHUNK = 16
BATCH = 8


def flat_device(x, y, z, core):
    return (y * 8 + (z // 4) * 4 + x) * 8 + (z % 4) * 2 + core


def ring_xz():
    ring = []
    for z in range(8):
        ring += [(x, z) for x in ((1, 2, 3) if z % 2 == 0 else (3, 2, 1))]
    return ring + [(0, z) for z in range(7, -1, -1)]


RING = ring_xz()


def home(w, n):
    return (w % WIDE) * NARROW + n % NARROW


def work(w, n):
    x, z = RING[w % WIDE]
    n = n % NARROW
    return flat_device(x, n if n < 4 else 7 - n, z, 0 if n < 4 else 1)


def send(shard, p=0, s=0, source=work, target=work):
    pairs = [
        (source(w, n), target(w + p, n + s)) for w in range(WIDE) for n in range(NARROW)
    ]
    return lax.ppermute(shard, AXES, pairs)


def device_of(index):
    w, n = divmod(index, NARROW)
    return (w % 4, w // 8, (w // 4) % 2 * 4 + n // 2, n % 2)


def flip_max(value, *flips):
    for flip in flips:
        pairs = []
        for index in range(WIDE * NARROW):
            place = device_of(index)
            pairs.append((index, flat_device(*(a ^ b for a, b in zip(place, flip)))))
        value = jnp.maximum(value, lax.ppermute(value, AXES, pairs))
    return value


def rank_rows(flags):
    rows = flags.shape[0]
    a = lax.broadcasted_iota(jnp.int32, (128, 128), 0)
    b = lax.broadcasted_iota(jnp.int32, (128, 128), 1)
    inside = jnp.dot(
        flags.astype(jnp.bfloat16), (a < b).astype(jnp.bfloat16),
        preferred_element_type=jnp.float32,
    )
    a = lax.broadcasted_iota(jnp.int32, (rows, rows), 0)
    b = lax.broadcasted_iota(jnp.int32, (rows, rows), 1)
    totals = jnp.sum(flags, axis=1, keepdims=True)
    before = jnp.dot(
        (b < a).astype(jnp.bfloat16), jnp.broadcast_to(totals, (rows, 128)).astype(jnp.bfloat16),
        preferred_element_type=jnp.float32,
    )
    return jnp.where(flags > 0, inside + before, -1.0), totals


def compact(candidates, capacity, spare):
    flags = jnp.concatenate([c[0] for c in candidates], axis=0)
    first = jnp.concatenate([c[1] for c in candidates], axis=0)
    second = jnp.concatenate([c[2] for c in candidates], axis=0)
    ranks, totals = rank_rows(flags)
    slots = lax.broadcasted_iota(jnp.int32, (capacity, 128), 0).astype(jnp.float32)
    result = jnp.zeros((16, capacity), jnp.float32)
    for row in range(flags.shape[0]):
        hits = (slots == ranks[row:row + 1]).astype(jnp.bfloat16)
        values = jnp.concatenate(
            [jnp.broadcast_to(first[row:row + 1], (8, 128)),
             jnp.broadcast_to(second[row:row + 1], (8, 128))], axis=0
        ).astype(jnp.bfloat16)
        result = result + lax.dot_general(
            values, hits, (((1,), (1,)), ((), ())), preferred_element_type=jnp.float32
        )
    index = lax.broadcasted_iota(jnp.int32, (8, capacity), 1)
    codes = (result[0:8] * 256.0 + result[8:16]).astype(jnp.int32)
    count = jnp.sum(totals)
    return jnp.where(index < count.astype(jnp.int32), codes, 16 * 256 + spare)[0:1], count


def split_list(listed):
    local, source = listed[0:2], listed[2:4]
    slot = jnp.floor(source * (1.0 / 16.0))
    return local, slot, source - 16.0 * slot


def flag(condition):
    return jnp.where(condition, 1.0, 0.0)


def near_tasks(own_ref, behind_ref, tasks_ref, counts_ref):
    local, slot, tile = split_list(own_ref[...])
    inner = flag(slot == 0.0)
    diagonal = inner * flag(local == tile)
    b_local, b_slot, b_tile = split_list(behind_ref[...])
    plain_tasks, plain = compact(
        [
            (inner - diagonal, local, tile),
            (inner - diagonal, tile, local),
            (flag(slot == 4.0), local, 32.0 + tile),
            (flag(b_slot == 4.0), b_tile, 16.0 + b_local),
        ],
        NEAR_TASKS, 0,
    )
    self_tasks, selves = compact([(diagonal, local, tile)], 128, 0)
    tasks_ref[...] = jnp.concatenate([plain_tasks, self_tasks], axis=1)
    lane = lax.broadcasted_iota(jnp.int32, (8, 128), 1)
    counts_ref[...] = jnp.where(lane == 0, plain, selves).astype(jnp.int32)


def far_tasks(own_ref, behind_ref, tasks_ref, counts_ref):
    local, slot, tile = split_list(own_ref[...])
    ahead = flag(slot >= 1.0) * flag(slot <= 3.0)
    candidates = [(ahead, local, (5.0 + slot) * 16.0 + tile)]
    for brick, want in ((3, 3.0), (4, 2.0), (5, 1.0)):
        b_local, b_slot, b_tile = split_list(behind_ref[brick - 3])
        candidates.append((flag(b_slot == want), b_tile, 16.0 * brick + b_local))
    tasks, count = compact(candidates, FAR_TASKS, 48)
    tasks_ref[...] = tasks
    counts_ref[...] = jnp.broadcast_to(count, (8, 128)).astype(jnp.int32)


NEAR_TASKS = 640
FAR_TASKS = 1152


def make_tasks(kernel, capacity, own_list, behind_list):
    return pl.pallas_call(
        kernel,
        out_shape=(
            jax.ShapeDtypeStruct((1, capacity), jnp.int32),
            jax.ShapeDtypeStruct((8, 128), jnp.int32),
        ),
        compiler_params=pltpu.CompilerParams(vmem_limit_bytes=32 * 1024 * 1024),
    )(own_list, behind_list)


def fill_rows(target, bricks, offsets, component):
    for brick, (value, offset) in enumerate(zip(bricks, offsets)):
        shifted = value * scale
        if component < 2 and offset[component] != 0:
            shifted = (value + brick_side * offset[component]) * scale
        target[pl.ds(brick * 16, 16), :] = shifted


def expand(rows, targets):
    blank = jnp.zeros((128 - rows.shape[0], 128), jnp.float32)
    columns = jnp.transpose(jnp.concatenate([rows, blank], axis=0))
    for component, target in enumerate(targets):
        for tile in range(16):
            lane = component * 16 + tile
            target[tile] = jnp.broadcast_to(columns[:, lane:lane + 1], (128, 128))
        target[16] = jnp.ones((128, 128), jnp.float32)


def collapse(sources):
    lanes = lax.broadcasted_iota(jnp.int32, (128, 128), 1)
    result = jnp.zeros((128, 128), jnp.float32)
    for component, source in enumerate(sources):
        for tile in range(16):
            total = jnp.sum(source[tile], axis=1, keepdims=True)
            result = jnp.where(lanes == component * 16 + tile, total, result)
    return jnp.transpose(result)[0:16 * len(sources)]


def loop_tasks(tasks, count, step):
    def visit(turn, carry):
        for lane in range(BATCH):
            code = tasks[0, turn * BATCH + lane]
            step(lax.shift_right_logical(code, 8), lax.bitwise_and(code, 255))
        return carry

    lax.fori_loop(0, lax.div(count + (BATCH - 1), BATCH), visit, 0)


def loop_single(tasks, begin, count, step):
    def visit(k, carry):
        code = tasks[0, begin + k]
        step(lax.shift_right_logical(code, 8), lax.bitwise_and(code, 255))
        return carry

    lax.fori_loop(0, count, visit, 0)


def not_self(begin):
    a = lax.broadcasted_iota(jnp.int32, (CHUNK, 128), 0) + begin
    b = lax.broadcasted_iota(jnp.int32, (CHUNK, 128), 1)
    return a != b


def screen_kernel(near, counts, tasks, own, radius, ghosts, ghost_radius, prior, out, scratch):
    gx, gy, gz, gr, ex, ey, ez, acc = scratch
    offsets = ghost_offsets[0:3] if near else ghost_offsets[3:9]
    for component, target in enumerate((gx, gy, gz)):
        rows = pl.ds(component * 16, 16)
        bricks = ([own[rows, :]] if near else []) + [ghost[rows, :] for ghost in ghosts]
        fill_rows(target, bricks, offsets, component)
    bricks = ([radius[...]] if near else []) + [ghost[...] for ghost in ghost_radius]
    for brick, value in enumerate(bricks):
        value = value * scale
        gr[pl.ds(brick * 16, 16), :] = value * value
    expand(own[...] * scale, (ex, ey, ez))
    acc[...] = jnp.zeros_like(acc)

    def step(masked, t, g):
        g = g if near else g - 48
        row = pl.ds(g, 1)
        bx, by, bz, br = gx[row, :], gy[row, :], gz[row, :], gr[row, :]
        for begin in range(0, 128, CHUNK):
            part = pl.ds(begin, CHUNK)
            dx = ex[t, part, :] - bx
            dy = ey[t, part, :] - by
            dz = ez[t, part, :] - bz
            u = dx * dx + dy * dy + dz * dz
            h = jnp.maximum(1.0 - u, 0.0)
            value = h * h * br * pl.reciprocal(u + br, approx=True)
            if masked:
                value = jnp.where(not_self(begin), value, 0.0)
            acc[t, part, :] += value

    if near:
        loop_single(tasks, NEAR_TASKS, counts[0, 1], functools.partial(step, True))
        loop_tasks(tasks, counts[0, 0], functools.partial(step, False))
        out[...] = collapse((acc,))
    else:
        loop_tasks(tasks, counts[0, 0], functools.partial(step, False))
        total = screen_factor * (collapse((acc,)) + prior[...])
        out[...] = radius[...] / (1.0 - 0.9 * jnp.tanh(total))


def force_kernel(near, counts, tasks, own, born, charge, ghosts, ghost_born, ghost_charge, extra,
                 outs, scratch):
    gx, gy, gz, gr, gk, gq, ex, ey, ez, er, ek, ax, ay, az = scratch
    offsets = ghost_offsets[0:3] if near else ghost_offsets[3:9]
    for component, target in enumerate((gx, gy, gz)):
        rows = pl.ds(component * 16, 16)
        bricks = ([own[rows, :]] if near else []) + [ghost[rows, :] for ghost in ghosts]
        fill_rows(target, bricks, offsets, component)
    bricks = ([born[...]] if near else []) + [ghost[...] for ghost in ghost_born]
    root = 1.25 * log2e ** 0.5
    for brick, value in enumerate(bricks):
        gr[pl.ds(brick * 16, 16), :] = value * scale
        gk[pl.ds(brick * 16, 16), :] = -root / value
    bricks = ([charge[...]] if near else []) + [ghost[...] for ghost in ghost_charge]
    for brick, value in enumerate(bricks):
        gq[pl.ds(brick * 16, 16), :] = value
    expand(
        jnp.concatenate([own[...] * scale, born[...] * scale, root / born[...]], axis=0),
        (ex, ey, ez, er, ek),
    )
    for acc in (ax, ay, az):
        acc[...] = jnp.zeros_like(acc)

    def step(masked, t, g):
        g = g if near else g - 48
        row = pl.ds(g, 1)
        bx, by, bz = gx[row, :], gy[row, :], gz[row, :]
        br, bk, bq = gr[row, :], gk[row, :], gq[row, :]
        for begin in range(0, 128, CHUNK):
            part = pl.ds(begin, CHUNK)
            dx = ex[t, part, :] - bx
            dy = ey[t, part, :] - by
            dz = ez[t, part, :] - bz
            u = dx * dx + dy * dy + dz * dz
            h = jnp.maximum(1.0 - u, 0.0)
            e = jnp.exp2(u * (ek[t, part, :] * bk))
            inverse = lax.rsqrt(u + er[t, part, :] * br * e)
            w = h * inverse
            c = (bq * w) * (16.0 + (4.0 - e) * (w * inverse))
            if masked:
                c = jnp.where(not_self(begin), c, 0.0)
            ax[t, part, :] += c * dx
            ay[t, part, :] += c * dy
            az[t, part, :] += c * dz

    if near:
        loop_single(tasks, NEAR_TASKS, counts[0, 1], functools.partial(step, True))
        loop_tasks(tasks, counts[0, 0], functools.partial(step, False))
        outs[0][...] = collapse((ax, ay, az))
    else:
        loop_tasks(tasks, counts[0, 0], functools.partial(step, False))
        prior, velocity, anchor = extra
        total = collapse((ax, ay, az)) + prior[...]
        q = jnp.concatenate([charge[...]] * 3, axis=0)
        v = velocity[...] + step_time * (-0.02 * (q * total))
        x = own[...] + step_time * v
        moved = x - anchor[...]
        squared = moved * moved
        squared = squared[0:16] + squared[16:32] + squared[32:48]
        outs[0][...] = x
        outs[1][...] = v
        outs[2][...] = jnp.broadcast_to(jnp.max(jnp.sqrt(squared)), (8, 128))


def vmem(rows=None):
    return pl.BlockSpec(memory_space=pltpu.VMEM)


def smem():
    return pl.BlockSpec(memory_space=pltpu.SMEM)


def params():
    return pltpu.CompilerParams(vmem_limit_bytes=40 * 1024 * 1024)


def tile_scratch(count):
    return [pltpu.VMEM((17, 128, 128), jnp.float32) for _ in range(count)]


def row_scratch(count, bricks):
    return [pltpu.VMEM((bricks * 16, 128), jnp.float32) for _ in range(count)]


def cost(flops):
    return pl.CostEstimate(flops=flops, bytes_accessed=1 << 20, transcendentals=flops // 16)


def screen(near, counts, tasks, own, radius, ghosts, ghost_radius, prior=None):
    many = len(ghosts)
    extra = [] if near else [prior]

    def kernel(*refs):
        counts, tasks, own, radius = refs[0:4]
        ghosts, ghost_radius = refs[4:4 + many], refs[4 + many:4 + 2 * many]
        rest = refs[4 + 2 * many:]
        prior, rest = (None, rest) if near else (rest[0], rest[1:])
        screen_kernel(near, counts, tasks, own, radius, ghosts, ghost_radius, prior, rest[0],
                      rest[1:])

    bricks = 3 if near else 6
    return pl.pallas_call(
        kernel,
        out_shape=jax.ShapeDtypeStruct((16, 128), jnp.float32),
        in_specs=[smem(), smem()] + [vmem()] * (2 + 2 * many + len(extra)),
        out_specs=vmem(),
        scratch_shapes=row_scratch(4, bricks) + tile_scratch(4),
        compiler_params=params(),
        cost_estimate=cost(1 << 26),
    )(counts, tasks, own, radius, *ghosts, *ghost_radius, *extra)


def force(near, counts, tasks, own, born, charge, ghosts, ghost_born, ghost_charge, extra=()):
    many = len(ghosts)

    def kernel(*refs):
        counts, tasks, own, born, charge = refs[0:5]
        rest = refs[5:]
        ghosts, ghost_born, ghost_charge = (
            rest[0:many], rest[many:2 * many], rest[2 * many:3 * many]
        )
        rest = rest[3 * many:]
        extras, rest = rest[0:len(extra)], rest[len(extra):]
        outs = 1 if near else 3
        force_kernel(near, counts, tasks, own, born, charge, ghosts, ghost_born, ghost_charge,
                     extras, rest[0:outs], rest[outs:])

    bricks = 3 if near else 6
    rows = jax.ShapeDtypeStruct((48, 128), jnp.float32)
    out_shape = (rows,) if near else (rows, rows, jax.ShapeDtypeStruct((8, 128), jnp.float32))
    return pl.pallas_call(
        kernel,
        out_shape=out_shape,
        in_specs=[smem(), smem()] + [vmem()] * (3 + 3 * many + len(extra)),
        out_specs=tuple(vmem() for _ in out_shape),
        scratch_shapes=row_scratch(6, bricks) + tile_scratch(8),
        compiler_params=params(),
        cost_estimate=cost(1 << 27),
    )(counts, tasks, own, born, charge, *ghosts, *ghost_born, *ghost_charge, *extra)


def slots_kernel(targets, out):
    codes = targets[...]
    result = jnp.full((16, 128), -1.0, jnp.float32)
    for heading in range(1, 9):
        flags = flag(codes == float(heading))
        ranks, totals = rank_rows(flags)
        result = jnp.where(flags > 0, ranks + float(MIGRANTS * (heading - 1)), result)
    out[...] = result


def migrant_slots(targets):
    return pl.pallas_call(
        slots_kernel, out_shape=jax.ShapeDtypeStruct((16, 128), jnp.float32)
    )(targets)


def pack_kernel(slots, position, velocity, out):
    def parts(value):
        high = value.astype(jnp.bfloat16)
        left = value - high.astype(jnp.float32)
        middle = left.astype(jnp.bfloat16)
        low = (left - middle.astype(jnp.float32)).astype(jnp.bfloat16)
        return high.astype(jnp.float32), middle.astype(jnp.float32), low.astype(jnp.float32)

    split = parts(position[...]), parts(velocity[...])
    wanted = lax.broadcasted_iota(jnp.int32, (8 * MIGRANTS, 128), 0).astype(jnp.float32)
    result = jnp.zeros((32, 8 * MIGRANTS), jnp.float32)
    blank = jnp.zeros((2, 128), jnp.float32)
    for tile in range(16):
        hits = (wanted == slots[tile:tile + 1, :]).astype(jnp.bfloat16)
        rows = []
        for piece in range(3):
            for kind in range(2):
                for component in range(3):
                    row = component * 16 + tile
                    rows.append(split[kind][piece][row:row + 1])
            rows.append(blank)
        rows.append(jnp.zeros((8, 128), jnp.float32))
        state = jnp.concatenate(rows, axis=0).astype(jnp.bfloat16)
        result = result + lax.dot_general(
            state, hits, (((1,), (1,)), ((), ())), preferred_element_type=jnp.float32
        )
    out[...] = (result[0:8] + result[8:16]) + result[16:24]


def pack_migrants(slots, position, velocity):
    table = pl.pallas_call(
        pack_kernel,
        out_shape=jax.ShapeDtypeStruct((8, 8 * MIGRANTS), jnp.float32),
        compiler_params=params(),
    )(slots, position, velocity)
    return jnp.transpose(table[0:6].reshape(6, 8, MIGRANTS), (1, 0, 2))


def across(value):
    return send(value, 0, 1), send(value, 0, -1)


def along(value):
    return send(value, 1, 0), send(value, -1, 0)


def body(positions, velocities, charges, radii, tile_pairs, tile_counts, destinations):
    live = jnp.arange(tile_pairs.shape[3], dtype=jnp.int32) < tile_counts[0, 0]
    listed = jnp.where(live[None], tile_pairs[0, 0], -1).astype(jnp.float32).reshape(4, 128)
    first = jnp.concatenate(
        [
            positions.reshape(48, 128),
            charges.reshape(16, 128),
            radii.reshape(16, 128),
            listed,
            jnp.zeros((4, 128), jnp.float32),
            velocities.reshape(48, 128),
            destinations.reshape(16, 128).astype(jnp.float32),
        ]
    )
    first = send(first, source=home)
    first, later = first[0:88], first[88:152]
    coords = anchor = first[0:48]
    charge, radius, own_list = first[48:64], first[64:80], first[80:84]
    velocity = later[0:48]
    slots = migrant_slots(later[48:64])

    shifts = []
    for moment in range(STEPS):
        message = first if moment == 0 else coords
        lower, upper = across(message)
        row = jnp.stack([lower, message, upper])
        behind, ahead = along(row)
        if moment == 0:
            near_charge = (lower[48:64], upper[48:64])
            near_radius = (lower[64:80], upper[64:80])
            near_list = make_tasks(near_tasks, NEAR_TASKS + 128, own_list, lower[80:84])
            far_charge = tuple(block[k, 48:64] for block in (behind, ahead) for k in range(3))
            far_radius = tuple(block[k, 64:80] for block in (behind, ahead) for k in range(3))
            far_list = make_tasks(far_tasks, FAR_TASKS, own_list, behind[:, 80:84])
            near_list = (near_list[1], near_list[0])
            far_list = (far_list[1], far_list[0])
        near = (lower[0:48], upper[0:48])
        far = tuple(block[k, 0:48] for block in (behind, ahead) for k in range(3))
        partial = screen(True, *near_list, coords, radius, near, near_radius)
        born = screen(False, *far_list, coords, radius, far, far_radius, partial)
        born_lower, born_upper = across(born)
        row = jnp.stack([born_lower, born, born_upper])
        behind, ahead = along(row)
        far_born = tuple(block[k] for block in (behind, ahead) for k in range(3))
        (partial,) = force(
            True, *near_list, coords, born, charge, near, (born_lower, born_upper), near_charge
        )
        coords, velocity, moved = force(
            False, *far_list, coords, born, charge, far, far_born, far_charge,
            (partial, velocity, anchor),
        )
        shifts.append(moved[0:1])
        if moment == 0:
            slots, velocity = lax.optimization_barrier((slots, velocity))

    outgoing = pack_migrants(slots, coords, velocity)
    shift = jnp.concatenate(shifts, axis=0)
    outgoing, shift = lax.optimization_barrier((outgoing, shift))
    back, forth = send(outgoing[0:3], -1, 0), send(outgoing[5:8], 1, 0)
    shift = flip_max(shift, (0, 0, 0, 1))
    back, forth, shift = lax.optimization_barrier((back, forth, shift))
    down = send(jnp.stack([back[0], outgoing[3], forth[0]]), 0, -1)
    up = send(jnp.stack([back[2], outgoing[4], forth[2]]), 0, 1)
    shift = flip_max(shift, (1, 0, 0, 0))
    down, up, shift = lax.optimization_barrier((down, up, shift))
    arrivals = jnp.stack([down[0], back[1], up[0], down[1], up[1], down[2], forth[1], up[2]])
    rest = jnp.concatenate([coords, velocity, born, arrivals.reshape(24, 128)])
    rest = send(rest, target=home)
    shift = flip_max(shift, (2, 0, 0, 0), (0, 1, 0, 0), (0, 2, 0, 0))
    rest, shift = lax.optimization_barrier((rest, shift))
    shift = flip_max(shift, (0, 0, 1, 0), (0, 0, 2, 0), (0, 0, 4, 0))
    shift = shift[:, 0] / skin_depth
    arrivals = rest[112:136].reshape(8, 6, MIGRANTS)
    return (
        rest[0:48].reshape(1, 1, 3, 2048),
        rest[48:96].reshape(1, 1, 3, 2048),
        rest[96:112].reshape(1, 1, 2048),
        arrivals[None, None],
        shift,
    )


def solution(mesh):
    in_specs = (
        P("wide", "narrow", None, None),
        P("wide", "narrow", None, None),
        P("wide", "narrow", None),
        P("wide", "narrow", None),
        P("wide", "narrow", None, None),
        P("wide", "narrow"),
        P("wide", "narrow", None),
    )
    out_specs = (
        P("wide", "narrow", None, None),
        P("wide", "narrow", None, None),
        P("wide", "narrow", None),
        P("wide", "narrow", None, None, None),
        P(),
    )
    return jax.shard_map(body, mesh=mesh, in_specs=in_specs, out_specs=out_specs, check_vma=False)
```
